512 devices in a mesh: row: 32 (over z, x_lo), col: 16 (over y, x_hi, core).
Axes of the slice: x: 4 (x_hi: 2, x_lo: 2; x = x_hi * 2 + x_lo), y: 4, z: 16, core: 2. Of those that a mesh axis runs over, the one named last changes fastest.
Arguments:
- q_stream: bfloat16 [4096, 4096], P('col', 'row'), may hold values from -6 to 6
- k_stream: bfloat16 [4096, 4096], P('col', 'row'), may hold values from -6 to 6
- v_stream: bfloat16 [4096, 4096], P('col', 'row'), may hold values from -6 to 6
- long_filter: float32 [4096, 4096], P(('col', 'row')), may hold values from -1.3 to 1.3
- skip_gain: float32 [4096], P(('col', 'row')), may hold values from -4 to 4
- residual: bfloat16 [4096, 4096], P('col', 'row'), may hold values from -24 to 24
- norm_gain: float32 [4096], replicated, may hold values from 0.5 to 1.5
- w_out: bfloat16 [4096, 4096], P('row', 'col'), may hold values from -0.09375 to 0.09375
- w_gate: bfloat16 [4096, 8192], P('row', 'col'), may hold values from -0.09375 to 0.09375
- w_up: bfloat16 [4096, 8192], P('row', 'col'), may hold values from -0.09375 to 0.09375
- w_down: bfloat16 [8192, 4096], P('col'), may hold values from -0.09375 to 0.09375
Outputs:
- block_out: bfloat16 [4096, 4096], P('col', 'row')
The draws below stay inside these ranges and needn't reach their ends.
All inputs are finite; a program needn't handle non-finite values.
Results may differ from the reference program's by a relative error of at most 0.015.
Values may be sent and summed in bfloat16 or wider, within the bound.
No kernel may reach another device: no remote copies, remote signals or barrier semaphores. Data moves between devices by JAX's collectives and lax.ppermute only.
A program may use at most 64 MiB of HBM per device.

```python
import math
import jax
import jax.numpy as jnp
from jax import lax

D = 4096
FFW = 8192
TOKENS = 4096


def draw_long_filter(key, part):
    key = jax.random.fold_in(key, 11)
    first_key, second_key = jax.random.split(key)
    position = jnp.arange(TOKENS, dtype=jnp.float32)[None, :]
    decay_len = jnp.exp(jax.random.uniform(first_key, (D, 1), jnp.float32, math.log(30.0), math.log(4.0 * TOKENS)))
    noise = jnp.clip(jax.random.normal(second_key, (D, TOKENS), jnp.float32), -5.0, 5.0)
    factor = jnp.sqrt(jnp.expm1(-2.0 / decay_len) / jnp.expm1(-2.0 * TOKENS / decay_len))
    return noise * jnp.exp(-position / decay_len) * factor


def draw_residual(key, part):
    key = jax.random.fold_in(key, 23)
    first_key, second_key = jax.random.split(key)
    feature = jnp.arange(D, dtype=jnp.float32)[:, None] / D
    feature_scale = 0.2 * jnp.exp(math.log(10.0) * feature)
    token_scale = jnp.exp(jax.random.uniform(first_key, (1, TOKENS), jnp.float32, math.log(0.3), math.log(3.0)))
    noise = jnp.clip(jax.random.normal(second_key, (D, TOKENS), jnp.float32), -4.0, 4.0)
    return (noise * feature_scale * token_scale).astype(jnp.bfloat16)


def with_spikes(array, key, source, target, parts, factor):
    owner, partner = [(jnp.arange(array.shape[dim]) // (array.shape[dim] // parts)).reshape([-1 if axis == dim else 1 for axis in range(array.ndim)]) for dim in (source, target)]
    chosen = jax.random.permutation(key, parts)[partner]
    strong = (owner == chosen) | (owner == (partner + parts // 2) % parts)
    return jnp.where(strong, factor * array, array)


def shard_levels(rng, extent, cuts, low, top_value):
    def one(dim, parts):
        draws = jax.random.uniform(jax.random.fold_in(jax.random.fold_in(rng, 6), dim), (parts,), jnp.float32, low / len(cuts), top_value / len(cuts))
        return jnp.repeat(jnp.exp(draws), extent[dim] // parts).reshape((-1,) + (1,) * (len(extent) - dim - 1))

    factor_of = one(*cuts[0])
    for cut in cuts[1:]:
        factor_of = factor_of * one(*cut)
    return factor_of


def gaussian(stream_key, extent, scale, limit, shards=(), kind=jnp.bfloat16):
    values = jax.random.normal(stream_key, extent, jnp.float32) * scale
    if len(shards) > 0:
        values = shard_levels(stream_key, extent, shards, -0.22, 0.18) * values
    return jnp.clip(values, min=-limit, max=limit).astype(kind)


def heavy_noise(rng, dims, width, bound, cuts, heavy, held_as=jnp.bfloat16):
    result = width * jax.random.normal(rng, dims, jnp.float32)
    if cuts:
        result = result * shard_levels(rng, dims, cuts, -0.22, 0.18)
    return jnp.clip(with_spikes(result, jax.random.fold_in(rng, 3), *heavy), -bound, bound).astype(held_as)


def setup_inputs(seed: int = 0) -> dict:
    arg_keys = jax.random.split(jax.random.key(seed), 12)
    return {
        "q_stream": gaussian(arg_keys[0], (D, TOKENS), 1.0, 6.0, ((0, 16), (1, 32))),
        "k_stream": gaussian(arg_keys[1], (D, TOKENS), 1.0, 6.0, ((0, 16), (1, 32))),
        "v_stream": gaussian(arg_keys[2], (D, TOKENS), 1.0, 6.0, ((0, 16), (1, 32))),
        "long_filter": draw_long_filter(jax.random.fold_in(arg_keys[11], 71), 0),
        "skip_gain": gaussian(arg_keys[4], (D,), 1.0, 4.0, ((0, 512),), jnp.float32),
        "residual": draw_residual(jax.random.fold_in(arg_keys[11], 71), 0),
        "norm_gain": jnp.clip(1.0 + 0.1 * jax.random.normal(arg_keys[6], (D,), jnp.float32), 0.5, 1.5),
        "w_out": gaussian(arg_keys[7], (D, D), D ** -0.5, 0.09375, ((0, 32), (1, 16))),
        "w_gate": gaussian(arg_keys[8], (D, FFW), D ** -0.5, 0.09375, ((0, 32), (1, 16))),
        "w_up": gaussian(arg_keys[9], (D, FFW), D ** -0.5, 0.09375, ((0, 32), (1, 16))),
        "w_down": heavy_noise(arg_keys[10], (FFW, D), FFW ** -0.5, 0.09375, ((0, 16),), (0, 1, 16, 2.0)),
    }


EPSILON = 1e-05

def causal_gate(inputs):
    query, keys_in, values_in, taps, skip_part = inputs
    product = keys_in.astype(jnp.float32) * values_in.astype(jnp.float32)
    positions = product.shape[1]
    span = 2 * positions
    spectrum = jnp.fft.rfft(product, n=span, axis=1) * jnp.fft.rfft(taps, n=span, axis=1)
    convolved = jnp.fft.irfft(spectrum, n=span, axis=1)[:, :positions]
    return (query.astype(jnp.float32) * (convolved + skip_part[:, None] * product)).astype(jnp.bfloat16)

def reference(q_stream, k_stream, v_stream, long_filter, skip_gain, residual, norm_gain, w_out, w_gate, w_up, w_down):
    groups = D // 256
    stacked = (q_stream.reshape(groups, 256, TOKENS), k_stream.reshape(groups, 256, TOKENS), v_stream.reshape(groups, 256, TOKENS), long_filter.reshape(groups, 256, TOKENS), skip_gain.reshape(groups, 256))
    gated_all = lax.map(causal_gate, stacked).reshape(D, TOKENS)
    mixed_out = jnp.dot(w_out.T, gated_all, preferred_element_type=jnp.float32)
    stream = (residual.astype(jnp.float32) + mixed_out).astype(jnp.bfloat16)
    power_sum = lax.optimization_barrier(jnp.sum(jnp.square(stream.astype(jnp.float32)), axis=0))
    inverse_rms = lax.rsqrt(power_sum / D + EPSILON)
    normed = (stream.astype(jnp.float32) * inverse_rms[None, :] * norm_gain[:, None]).astype(jnp.bfloat16)
    gate_proj = jnp.dot(w_gate.T, normed, preferred_element_type=jnp.float32)
    up_proj = jnp.dot(w_up.T, normed, preferred_element_type=jnp.float32)
    hidden = (jax.nn.silu(gate_proj) * up_proj).astype(jnp.bfloat16)
    down_out = jnp.dot(w_down.T, hidden, preferred_element_type=jnp.float32)
    return (stream.astype(jnp.float32) + down_out).astype(jnp.bfloat16)
```

```python
import math

import jax
import jax.numpy as jnp
from jax import lax
from jax.sharding import Mesh
from jax.sharding import PartitionSpec as P

EPSILON = 1e-05
TWO_PI = 2.0 * math.pi
ROW = ("z", "xl")
COL = ("y", "xh", "core")
PLANE = ("xl", "y", "xh", "core")


def contract(left_side, right_side):
    return lax.dot_general(
        left_side, right_side, (((0,), (0,)), ((), ())), preferred_element_type=jnp.float32
    )


def dft_tables(length):
    span = 2 * length
    tall = span // 128
    half_rows = length // 128
    k_first = jnp.arange(tall, dtype=jnp.int32)[:, None]
    n_first = jnp.arange(half_rows, dtype=jnp.int32)[None, :]
    angle_first = (k_first * n_first % tall).astype(jnp.float32) * (TWO_PI / tall)
    n_second = jnp.arange(128, dtype=jnp.int32)[None, :]
    angle_twist = (k_first * n_second % span).astype(jnp.float32) * (TWO_PI / span)
    k_second = jnp.arange(128, dtype=jnp.int32)
    angle_second = (k_second[:, None] * k_second[None, :] % 128).astype(jnp.float32) * (
        TWO_PI / 128
    )
    return (
        jnp.cos(angle_first),
        -jnp.sin(angle_first),
        jnp.cos(angle_twist),
        -jnp.sin(angle_twist),
        jnp.cos(angle_second),
        -jnp.sin(angle_second),
    )


def apply_first(matrix, blocks):
    return jnp.einsum("kn,cnm->ckm", matrix, blocks, precision=lax.Precision.HIGHEST)


def apply_last(blocks, matrix):
    return jnp.einsum("ckn,nm->ckm", blocks, matrix, precision=lax.Precision.HIGHEST)


def apply_back(matrix, blocks):
    return jnp.einsum("kn,ckm->cnm", matrix, blocks, precision=lax.Precision.HIGHEST)


def forward_dft(signal, tables):
    cos_first, sin_first, twist_re, twist_im, cos_second, sin_second = tables
    blocks = signal.reshape(signal.shape[0], signal.shape[1] // 128, 128)
    first_re = apply_first(cos_first, blocks)
    first_im = apply_first(sin_first, blocks)
    turned_re = first_re * twist_re - first_im * twist_im
    turned_im = first_re * twist_im + first_im * twist_re
    spec_re = apply_last(turned_re, cos_second) - apply_last(turned_im, sin_second)
    spec_im = apply_last(turned_re, sin_second) + apply_last(turned_im, cos_second)
    return (spec_re, spec_im)


def inverse_dft(spec_re, spec_im, tables, length):
    cos_first, sin_first, twist_re, twist_im, cos_second, sin_second = tables
    back_re = apply_last(spec_re, cos_second) + apply_last(spec_im, sin_second)
    back_im = apply_last(spec_im, cos_second) - apply_last(spec_re, sin_second)
    turned_re = back_re * twist_re + back_im * twist_im
    turned_im = back_im * twist_re - back_re * twist_im
    signal = (apply_back(cos_first, turned_re) + apply_back(sin_first, turned_im)) / (2.0 * length)
    return signal.reshape(signal.shape[0], length)


def to_plane(tile):
    halves = tile.reshape(2, 1, 128, 128)
    spread = jnp.broadcast_to(halves, (2, 16, 128, 128)).reshape(32, 128, 128)
    parts = lax.all_to_all(spread, PLANE, split_axis=0, concat_axis=0, tiled=True)
    return parts.reshape(2, 2048, 128)


def swap(array):
    return lax.ppermute(array, "xl", [(0, 1), (1, 0)])


def on_device(
    q_stream,
    k_stream,
    v_stream,
    long_filter,
    skip_gain,
    residual,
    norm_gain,
    w_out,
    w_gate,
    w_up,
    w_down,
):
    mine = lax.axis_index("xl")
    weights = lax.all_gather(
        jnp.concatenate([w_out, w_gate, w_up], axis=1), "z", axis=0, tiled=True
    )
    product = (k_stream.astype(jnp.float32) * v_stream.astype(jnp.float32)).astype(jnp.bfloat16)
    signal = lax.all_to_all(product, ROW, split_axis=0, concat_axis=1, tiled=True)
    length = signal.shape[1]
    tables = dft_tables(length)
    taps = jnp.concatenate([long_filter[:, :1] + skip_gain[:, None], long_filter[:, 1:]], axis=1)
    filter_re, filter_im = forward_dft(taps, tables)
    signal_re, signal_im = forward_dft(signal.astype(jnp.float32), tables)
    joint_re = signal_re * filter_re - signal_im * filter_im
    joint_im = signal_re * filter_im + signal_im * filter_re
    convolved = inverse_dft(joint_re, joint_im, tables, length).astype(jnp.bfloat16)
    convolved = lax.all_to_all(convolved, ROW, split_axis=1, concat_axis=0, tiled=True)
    gated = (q_stream.astype(jnp.float32) * convolved.astype(jnp.float32)).astype(jnp.bfloat16)
    gated_plane = to_plane(gated)
    weight_mix = weights[:, :256]
    far = contract(weight_mix, lax.dynamic_index_in_dim(gated_plane, 1 - mine, 0, keepdims=False))
    far = swap(far)
    near = contract(weight_mix, lax.dynamic_index_in_dim(gated_plane, mine, 0, keepdims=False))
    stream = (residual.astype(jnp.float32) + (near + far)).astype(jnp.bfloat16)
    stream_plane = to_plane(stream)
    wide = stream_plane.astype(jnp.float32)
    power = jnp.sum(jnp.square(wide), axis=1)
    gains = lax.dynamic_index_in_dim(norm_gain.reshape(16, 2, 128), mine, 1, keepdims=False)
    scaled = (wide * gains.reshape(1, 2048, 1)).astype(jnp.bfloat16)
    weight_ffw = weights[:, 256:]
    power_far = swap(lax.dynamic_index_in_dim(power, 1 - mine, 0, keepdims=False))
    far = contract(weight_ffw, lax.dynamic_index_in_dim(scaled, 1 - mine, 0, keepdims=False))
    far = swap(far.astype(jnp.bfloat16))
    near = contract(weight_ffw, lax.dynamic_index_in_dim(scaled, mine, 0, keepdims=False))
    power_sum = lax.dynamic_index_in_dim(power, mine, 0, keepdims=False) + power_far
    inverse_rms = lax.rsqrt(power_sum / norm_gain.shape[0] + EPSILON)
    both = (near + far.astype(jnp.float32)) * inverse_rms[None, :]
    hidden = (jax.nn.silu(both[:512]) * both[512:]).astype(jnp.bfloat16)
    down = contract(w_down, hidden).astype(jnp.bfloat16).reshape(16, 256, 128)
    parts = lax.all_to_all(down, COL, split_axis=0, concat_axis=0, tiled=True)
    down_out = jnp.sum(parts.astype(jnp.float32), axis=0)
    return (stream.astype(jnp.float32) + down_out).astype(jnp.bfloat16)


def solution(mesh):
    fine = Mesh(mesh.devices.reshape(16, 2, 4, 2, 2), ("z", "xl", "y", "xh", "core"))
    placed = (
        P(COL, ROW),
        P(COL, ROW),
        P(COL, ROW),
        P(COL + ROW, None),
        P(COL + ROW),
        P(COL, ROW),
        P(),
        P(ROW, COL),
        P(ROW, COL),
        P(ROW, COL),
        P(COL, None),
    )
    return jax.shard_map(
        on_device, mesh=fine, in_specs=placed, out_specs=P(COL, ROW), check_vma=False
    )
```

```python
import math

import jax
import jax.numpy as jnp
from jax import lax
from jax.experimental import pallas as pl
from jax.experimental.pallas import tpu as pltpu
from jax.sharding import Mesh
from jax.sharding import PartitionSpec as P

EPSILON = 1e-05
TWO_PI = 2.0 * math.pi
ROW = ("z", "xl")
COL = ("y", "xh", "core")


def dft_tables(length):
    span = 2 * length
    tall = span // 128
    half_rows = length // 128
    k_first = jnp.arange(tall, dtype=jnp.int32)[:, None]
    n_first = jnp.arange(half_rows, dtype=jnp.int32)[None, :]
    angle_first = (k_first * n_first % tall).astype(jnp.float32) * (TWO_PI / tall)
    n_second = jnp.arange(128, dtype=jnp.int32)[None, :]
    angle_twist = (k_first * n_second % span).astype(jnp.float32) * (TWO_PI / span)
    k_second = jnp.arange(128, dtype=jnp.int32)
    angle_second = (k_second[:, None] * k_second[None, :] % 128).astype(jnp.float32) * (
        TWO_PI / 128
    )
    return (
        jnp.cos(angle_first),
        -jnp.sin(angle_first),
        jnp.cos(angle_twist),
        -jnp.sin(angle_twist),
        jnp.cos(angle_second),
        -jnp.sin(angle_second),
    )


def apply_first(matrix, blocks):
    return jnp.einsum("kn,cnm->ckm", matrix, blocks, precision=lax.Precision.HIGHEST)


def apply_last(blocks, matrix):
    return jnp.einsum("ckn,nm->ckm", blocks, matrix, precision=lax.Precision.HIGHEST)


def apply_back(matrix, blocks):
    return jnp.einsum("kn,ckm->cnm", matrix, blocks, precision=lax.Precision.HIGHEST)


def forward_dft(signal, tables):
    cos_first, sin_first, twist_re, twist_im, cos_second, sin_second = tables
    blocks = signal.reshape(signal.shape[0], signal.shape[1] // 128, 128)
    first_re = apply_first(cos_first, blocks)
    first_im = apply_first(sin_first, blocks)
    turned_re = first_re * twist_re - first_im * twist_im
    turned_im = first_re * twist_im + first_im * twist_re
    spec_re = apply_last(turned_re, cos_second) - apply_last(turned_im, sin_second)
    spec_im = apply_last(turned_re, sin_second) + apply_last(turned_im, cos_second)
    return (spec_re, spec_im)


def inverse_dft(spec_re, spec_im, tables, length):
    cos_first, sin_first, twist_re, twist_im, cos_second, sin_second = tables
    back_re = apply_last(spec_re, cos_second) + apply_last(spec_im, sin_second)
    back_im = apply_last(spec_im, cos_second) - apply_last(spec_re, sin_second)
    turned_re = back_re * twist_re + back_im * twist_im
    turned_im = back_im * twist_re - back_re * twist_im
    signal = (apply_back(cos_first, turned_re) + apply_back(sin_first, turned_im)) / (2.0 * length)
    return signal.reshape(signal.shape[0], length)


def swap(array, axis):
    return lax.ppermute(array, axis, [(0, 1), (1, 0)])


def after(array, *others):
    return lax.optimization_barrier((array,) + others)[0]


def to_plane(tile):
    halves = tile.reshape(128, 2, 128).transpose(1, 0, 2)[:, None]
    spread = jnp.broadcast_to(halves, (2, 8, 128, 128)).reshape(16, 128, 128)
    return lax.all_to_all(spread, ("xl", "y", "xh"), split_axis=0, concat_axis=0, tiled=True)


def both_tiles(parts_ref, side, index):
    far, near = (1 - side) * 8, side * 8
    return jnp.concatenate(
        [
            jnp.concatenate([parts_ref[far + index + i], parts_ref[near + index + i]], axis=0)
            for i in range(2)
        ],
        axis=1,
    )


def mix_kernel(where_ref, own_ref, other_ref, w_own_ref, w_other_ref, far_ref, near_ref):
    side = where_ref[1]
    total = jnp.zeros((256, 256), jnp.float32)
    for parts_ref, w_ref in ((own_ref, w_own_ref), (other_ref, w_other_ref)):
        for i in range(4):
            total += jnp.dot(
                both_tiles(parts_ref, side, 2 * i),
                w_ref[2 * i : 2 * i + 2].reshape(256, 256),
                preferred_element_type=jnp.float32,
            )
    far_ref[...] = total[:128]
    near_ref[...] = total[128:]


def half_ffw(side, parts_ref, gain_ref, w_ref):
    total = jnp.zeros((256, 1024), jnp.float32)
    power = jnp.zeros((256, 1), jnp.float32)
    for i in range(4):
        wide = both_tiles(parts_ref, side, 2 * i).astype(jnp.float32)
        power += jnp.sum(wide * wide, axis=1, keepdims=True)
        scaled = wide * gain_ref[:, i * 256 : i * 256 + 256]
        total += jnp.dot(
            scaled.astype(jnp.bfloat16),
            w_ref[2 * i : 2 * i + 2].reshape(256, 1024),
            preferred_element_type=jnp.float32,
        )
    return total, jnp.broadcast_to(power, (256, 128))


def first_kernel(where_ref, parts_ref, gain_ref, w_ref, total_ref, power_ref):
    total, power = half_ffw(where_ref[1], parts_ref, gain_ref, w_ref)
    total_ref[...] = total
    power_ref[...] = power


def second_kernel(
    where_ref, parts_ref, gain_ref, begun_ref, power_ref, w_ref, far_ref, near_ref, own_power_ref
):
    total, power = half_ffw(where_ref[1], parts_ref, gain_ref, w_ref)
    total += begun_ref[...]
    power += power_ref[...]
    far_ref[:128] = total[:128].astype(jnp.bfloat16)
    row = power[:128].T[:16]
    high = row.astype(jnp.bfloat16)
    low = (row - high.astype(jnp.float32)).astype(jnp.bfloat16)
    pair = jnp.concatenate([high, low], axis=1)
    far_ref[128:] = jnp.concatenate([pair, pair, pair, pair], axis=1)
    near_ref[...] = total[128:]
    own_power_ref[...] = power[128:]


def columns_of(w_ref, index, core):
    return w_ref[:, pl.ds(pl.multiple_of((2 * index + core) * 256, 256), 256)]


def down_far_kernel(where_ref, near_ref, far_ref, power_ref, w_ref, out_ref, hidden_ref):
    sums = far_ref[128:].astype(jnp.float32)
    sums = jnp.broadcast_to(sums[:1, :128] + sums[:1, 128:256], (128, 128)).T
    inverse_rms = lax.rsqrt((power_ref[:, :1] + sums[:, :1]) / 4096 + EPSILON)
    both = (near_ref[...] + far_ref[:128].astype(jnp.float32)) * inverse_rms
    hidden = (jax.nn.silu(both[:, :512]) * both[:, 512:]).astype(jnp.bfloat16)
    hidden_ref[...] = hidden
    for i in range(8):
        out_ref[i] = jnp.dot(
            hidden, columns_of(w_ref, i, 1 - where_ref[0]), preferred_element_type=jnp.float32
        ).astype(jnp.bfloat16)


def down_near_kernel(where_ref, hidden_ref, w_ref, out_ref):
    for i in range(8):
        out_ref[i] = jnp.dot(
            hidden_ref[...], columns_of(w_ref, i, where_ref[0]), preferred_element_type=jnp.float32
        )


def local_call(kernel, where, operands, outs, flops):
    outs = [jax.ShapeDtypeStruct(shape, dtype) for shape, dtype in outs]
    return pl.pallas_call(
        kernel,
        in_specs=[pl.BlockSpec(memory_space=pltpu.SMEM)]
        + [pl.BlockSpec(memory_space=pltpu.VMEM)] * len(operands),
        out_specs=[pl.BlockSpec(memory_space=pltpu.VMEM)] * len(outs),
        out_shape=outs,
        compiler_params=pltpu.CompilerParams(vmem_limit_bytes=16 * 1024 * 1024),
        cost_estimate=pl.CostEstimate(flops=flops, bytes_accessed=2**21, transcendentals=0),
    )(where, *operands)


def on_device(
    q_stream,
    k_stream,
    v_stream,
    long_filter,
    skip_gain,
    residual,
    norm_gain,
    w_out,
    w_gate,
    w_up,
    w_down,
):
    side = lax.axis_index("xl")
    core = lax.axis_index("core")
    where = jnp.stack([core, side]).astype(jnp.int32)
    weights = lax.all_gather(
        jnp.concatenate([w_gate, w_up, w_out], axis=1), "z", axis=0, tiled=True
    ).reshape(8, 2, 128, 1280)

    def rows_of(gathered, owner, start, width):
        part = lax.dynamic_slice(gathered, (0, owner, 0, start), (8, 1, 128, width))
        return part.reshape(8, 128, width)

    product = (k_stream.astype(jnp.float32) * v_stream.astype(jnp.float32)).astype(jnp.bfloat16)
    signal = lax.all_to_all(product, ROW, split_axis=0, concat_axis=1, tiled=True)
    length = signal.shape[1]
    tables = dft_tables(length)
    taps = jnp.concatenate([long_filter[:, :1] + skip_gain[:, None], long_filter[:, 1:]], axis=1)
    filter_re, filter_im = forward_dft(taps, tables)
    signal_re, signal_im = forward_dft(signal.astype(jnp.float32), tables)
    joint_re = signal_re * filter_re - signal_im * filter_im
    joint_im = signal_re * filter_im + signal_im * filter_re
    convolved = inverse_dft(joint_re, joint_im, tables, length).astype(jnp.bfloat16)
    convolved = lax.all_to_all(convolved, ROW, split_axis=1, concat_axis=0, tiled=True)
    gated = (q_stream.astype(jnp.float32) * convolved.astype(jnp.float32)).astype(jnp.bfloat16)
    own = to_plane(gated.T)
    other = swap(own, "core")
    far, near = local_call(
        mix_kernel,
        where,
        (own, other, rows_of(weights, core, 1024, 256), rows_of(weights, 1 - core, 1024, 256)),
        [((128, 256), jnp.float32)] * 2,
        2 * 256 * 256 * 2048,
    )
    weights = after(weights, near)
    w_own, w_other = rows_of(weights, core, 0, 1024), rows_of(weights, 1 - core, 0, 1024)
    far = swap(far, "xl")
    far = after(far, w_own, w_other)
    stream = (residual.T.astype(jnp.float32) + (near + far)).astype(jnp.bfloat16)
    own = to_plane(stream)
    other = swap(own, "core")
    gains = lax.dynamic_index_in_dim(norm_gain.reshape(8, 2, 2, 128), side, 2, keepdims=False)
    gain_own = lax.dynamic_index_in_dim(gains, core, 1, keepdims=False).reshape(1, 1024)
    gain_other = lax.dynamic_index_in_dim(gains, 1 - core, 1, keepdims=False).reshape(1, 1024)
    begun, power = local_call(
        first_kernel,
        where,
        (own, gain_own, w_own),
        [((256, 1024), jnp.float32), ((256, 128), jnp.float32)],
        2 * 256 * 1024 * 1024,
    )
    other = after(other, begun)
    far, near, power = local_call(
        second_kernel,
        where,
        (other, gain_other, begun, power, w_other),
        [((144, 1024), jnp.bfloat16), ((128, 1024), jnp.float32), ((128, 128), jnp.float32)],
        2 * 256 * 1024 * 1024,
    )
    far = swap(far, "xl")
    far, hidden = local_call(
        down_far_kernel,
        where,
        (near, far, power, w_down),
        [((8, 128, 256), jnp.bfloat16), ((128, 512), jnp.bfloat16)],
        2 * 128 * 512 * 2048,
    )
    far = swap(far, "core")
    (near,) = local_call(
        down_near_kernel,
        where,
        (hidden, w_down),
        [((8, 128, 256), jnp.float32)],
        2 * 128 * 512 * 2048,
    )
    far = after(far, near)
    down = (near + far.astype(jnp.float32)).astype(jnp.bfloat16)
    parts = lax.all_to_all(
        down,
        ("y", "xh"),
        split_axis=0,
        concat_axis=0,
        tiled=True,
    )
    down_out = jnp.sum(parts.astype(jnp.float32), axis=0)
    return (stream.astype(jnp.float32) + down_out).astype(jnp.bfloat16).T


def solution(mesh):
    fine = Mesh(mesh.devices.reshape(16, 2, 4, 2, 2), ("z", "xl", "y", "xh", "core"))
    placed = (
        P(COL, ROW),
        P(COL, ROW),
        P(COL, ROW),
        P(COL + ROW, None),
        P(COL + ROW),
        P(COL, ROW),
        P(),
        P(ROW, COL),
        P(ROW, COL),
        P(ROW, COL),
        P(COL, None),
    )
    return jax.shard_map(
        on_device, mesh=fine, in_specs=placed, out_specs=P(COL, ROW), check_vma=False
    )
```

```python
import math

import jax
import jax.numpy as jnp
from jax import lax
from jax.experimental import pallas as pl
from jax.experimental.pallas import tpu as pltpu
from jax.sharding import Mesh
from jax.sharding import PartitionSpec as P

EPSILON = 1e-05
TWO_PI = 2.0 * math.pi
ROW = ("z", "xl")
COL = ("y", "xh", "core")


def dft_tables(length):
    span = 2 * length
    tall = span // 128
    half_rows = length // 128
    k_first = jnp.arange(tall, dtype=jnp.int32)[:, None]
    n_first = jnp.arange(half_rows, dtype=jnp.int32)[None, :]
    angle_first = (k_first * n_first % tall).astype(jnp.float32) * (TWO_PI / tall)
    n_second = jnp.arange(128, dtype=jnp.int32)[None, :]
    angle_twist = (k_first * n_second % span).astype(jnp.float32) * (TWO_PI / span)
    k_second = jnp.arange(128, dtype=jnp.int32)
    angle_second = (k_second[:, None] * k_second[None, :] % 128).astype(jnp.float32) * (
        TWO_PI / 128
    )
    return (
        jnp.cos(angle_first),
        -jnp.sin(angle_first),
        jnp.cos(angle_twist),
        -jnp.sin(angle_twist),
        jnp.cos(angle_second),
        -jnp.sin(angle_second),
    )


def apply_first(matrix, blocks):
    return jnp.einsum("kn,cnm->ckm", matrix, blocks, precision=lax.Precision.HIGHEST)


def apply_last(blocks, matrix):
    return jnp.einsum("ckn,nm->ckm", blocks, matrix, precision=lax.Precision.HIGHEST)


def apply_back(matrix, blocks):
    return jnp.einsum("kn,ckm->cnm", matrix, blocks, precision=lax.Precision.HIGHEST)


def forward_dft(signal, tables):
    cos_first, sin_first, twist_re, twist_im, cos_second, sin_second = tables
    blocks = signal.reshape(signal.shape[0], signal.shape[1] // 128, 128)
    first_re = apply_first(cos_first, blocks)
    first_im = apply_first(sin_first, blocks)
    turned_re = first_re * twist_re - first_im * twist_im
    turned_im = first_re * twist_im + first_im * twist_re
    spec_re = apply_last(turned_re, cos_second) - apply_last(turned_im, sin_second)
    spec_im = apply_last(turned_re, sin_second) + apply_last(turned_im, cos_second)
    return (spec_re, spec_im)


def inverse_dft(spec_re, spec_im, tables, length):
    cos_first, sin_first, twist_re, twist_im, cos_second, sin_second = tables
    back_re = apply_last(spec_re, cos_second) + apply_last(spec_im, sin_second)
    back_im = apply_last(spec_im, cos_second) - apply_last(spec_re, sin_second)
    turned_re = back_re * twist_re + back_im * twist_im
    turned_im = back_im * twist_re - back_re * twist_im
    signal = (apply_back(cos_first, turned_re) + apply_back(sin_first, turned_im)) / (2.0 * length)
    return signal.reshape(signal.shape[0], length)


def swap(array, axis):
    return lax.ppermute(array, axis, [(0, 1), (1, 0)])


def after(array, *others):
    return lax.optimization_barrier((array,) + others)[0]


def gather_plane(spread):
    return lax.all_to_all(spread, ("xl", "y", "xh"), split_axis=0, concat_axis=0, tiled=True)


def mix_kernel(
    where_ref, own_ref, other_ref, residual_ref, w_own_ref, w_other_ref, out_ref, total_ref
):
    total = jnp.zeros((256, 256), jnp.float32)
    for parts_ref, w_ref in ((own_ref, w_own_ref), (other_ref, w_other_ref)):
        for i in range(0, 8, 2):
            rows = [
                jnp.concatenate([parts_ref[i + j], parts_ref[8 + i + j]], axis=0) for j in range(2)
            ]
            total += jnp.dot(
                jnp.concatenate(rows, axis=1),
                w_ref[i : i + 2].reshape(256, 256),
                preferred_element_type=jnp.float32,
            )
    total_ref[...] = total
    near = pl.ds(pl.multiple_of(where_ref[1] * 128, 128), 128)
    total_ref[near] = total_ref[near] + residual_ref[...].astype(jnp.float32)
    out_ref[0] = total_ref[:, :128].astype(jnp.bfloat16)
    out_ref[1] = total_ref[:, 128:].astype(jnp.bfloat16)


def half_ffw(tokens, parts_ref, gain_ref, w_ref):
    total, power = 0.0, 0.0
    for i in range(4):
        wide = jnp.concatenate([parts_ref[2 * i, tokens], parts_ref[2 * i + 1, tokens]], axis=1)
        wide = wide.astype(jnp.float32)
        power += jnp.sum(wide * wide, axis=1, keepdims=True)
        scaled = wide * gain_ref[:, i * 256 : i * 256 + 256]
        total += jnp.dot(
            scaled.astype(jnp.bfloat16),
            w_ref[2 * i : 2 * i + 2].reshape(256, 1024),
            preferred_element_type=jnp.float32,
        )
    return total, jnp.broadcast_to(power, (power.shape[0], 128))


def first_kernel(where_ref, parts_ref, gain_ref, w_ref, total_ref, power_ref):
    total_ref[...], power_ref[...] = half_ffw(pl.ds(0, 256), parts_ref, gain_ref, w_ref)


def far_kernel(
    where_ref, parts_ref, gain_ref, begun_ref, power_ref, own_ref, w_ref, out_ref
):
    far = pl.ds(pl.multiple_of((1 - where_ref[1]) * 128, 128), 128)
    total, power = half_ffw(far, parts_ref, gain_ref, w_ref)
    out_ref[:128] = (total + begun_ref[far]).astype(jnp.bfloat16)
    row = (power + power_ref[far]).T[:16]
    high = row.astype(jnp.bfloat16)
    low = (row - high.astype(jnp.float32)).astype(jnp.bfloat16)
    out_ref[128:144] = jnp.concatenate([high, low] * 4, axis=1)
    stream = own_ref[where_ref[2], far]
    out_ref[144:] = jnp.concatenate([stream[16 * i : 16 * i + 16] for i in range(8)], axis=1)


def near_kernel(
    where_ref, parts_ref, gain_ref, begun_ref, power_ref, w_ref, total_ref, own_power_ref
):
    near = pl.ds(pl.multiple_of(where_ref[1] * 128, 128), 128)
    total, power = half_ffw(near, parts_ref, gain_ref, w_ref)
    total_ref[...] = total + begun_ref[near]
    own_power_ref[...] = power + power_ref[near]


def columns_of(w_ref, index, core):
    return w_ref[:, pl.ds(pl.multiple_of((2 * index + core) * 256, 256), 256)]


def down_far_kernel(
    where_ref, near_ref, far_ref, power_ref, own_ref, w_ref, out_ref, hidden_ref, stream_ref
):
    sums = far_ref[128:144].astype(jnp.float32)
    sums = jnp.broadcast_to(sums[:1, :128] + sums[:1, 128:256], (128, 128)).T
    inverse_rms = lax.rsqrt((power_ref[:, :1] + sums[:, :1]) / 4096 + EPSILON)
    both = (near_ref[...] + far_ref[:128].astype(jnp.float32)) * inverse_rms
    hidden = (jax.nn.silu(both[:, :512]) * both[:, 512:]).astype(jnp.bfloat16)
    hidden_ref[...] = hidden
    for i in range(8):
        out_ref[i] = jnp.dot(
            hidden, columns_of(w_ref, i, 1 - where_ref[0]), preferred_element_type=jnp.float32
        ).astype(jnp.bfloat16)
    side = where_ref[1]
    packed = far_ref[144:]
    back = jnp.concatenate([packed[:, 128 * i : 128 * i + 128] for i in range(8)], axis=0)
    kept = own_ref[where_ref[2], pl.ds(pl.multiple_of(side * 128, 128), 128)]
    stream_ref[:, :128] = jnp.where(side == 0, kept, back)
    stream_ref[:, 128:] = jnp.where(side == 0, back, kept)


def down_near_kernel(where_ref, hidden_ref, w_ref, out_ref):
    for i in range(8):
        out_ref[i] = jnp.dot(
            hidden_ref[...], columns_of(w_ref, i, where_ref[0]), preferred_element_type=jnp.float32
        )


def local_call(kernel, where, operands, outs, flops, scratch=()):
    outs = [jax.ShapeDtypeStruct(shape, dtype) for shape, dtype in outs]
    return pl.pallas_call(
        kernel,
        in_specs=[pl.BlockSpec(memory_space=pltpu.SMEM)]
        + [pl.BlockSpec(memory_space=pltpu.VMEM)] * len(operands),
        out_specs=[pl.BlockSpec(memory_space=pltpu.VMEM)] * len(outs),
        out_shape=outs,
        scratch_shapes=scratch,
        compiler_params=pltpu.CompilerParams(vmem_limit_bytes=16 * 1024 * 1024),
        cost_estimate=pl.CostEstimate(flops=flops, bytes_accessed=2**21, transcendentals=0),
    )(where, *operands)


def on_device(
    q_stream,
    k_stream,
    v_stream,
    long_filter,
    skip_gain,
    residual,
    norm_gain,
    w_out,
    w_gate,
    w_up,
    w_down,
):
    side = lax.axis_index("xl")
    core = lax.axis_index("core")
    column = lax.axis_index(("y", "xh"))
    where = jnp.stack([core, side, column]).astype(jnp.int32)
    weights = lax.all_gather(
        jnp.concatenate([w_gate, w_up, w_out], axis=1), "z", axis=0, tiled=True
    ).reshape(8, 2, 128, 1280)

    def rows_of(gathered, owner, start, width):
        part = lax.dynamic_slice(gathered, (0, owner, 0, start), (8, 1, 128, width))
        return part.reshape(8, 128, width)

    product = (k_stream.astype(jnp.float32) * v_stream.astype(jnp.float32)).astype(jnp.bfloat16)
    signal = lax.all_to_all(product, ROW, split_axis=0, concat_axis=1, tiled=True)
    length = signal.shape[1]
    tables = dft_tables(length)
    taps = jnp.concatenate([long_filter[:, :1] + skip_gain[:, None], long_filter[:, 1:]], axis=1)
    filter_re, filter_im = forward_dft(taps, tables)
    signal_re, signal_im = forward_dft(signal.astype(jnp.float32), tables)
    joint_re = signal_re * filter_re - signal_im * filter_im
    joint_im = signal_re * filter_im + signal_im * filter_re
    convolved = inverse_dft(joint_re, joint_im, tables, length).astype(jnp.bfloat16)
    convolved = lax.all_to_all(convolved, ROW, split_axis=1, concat_axis=0, tiled=True)
    gated = (q_stream.astype(jnp.float32) * convolved.astype(jnp.float32)).astype(jnp.bfloat16)
    halves = gated.T.reshape(128, 2, 128).transpose(1, 0, 2)[:, None]
    own = gather_plane(jnp.broadcast_to(halves, (2, 8, 128, 128)).reshape(16, 128, 128))
    other = swap(own, "core")
    mixed = local_call(
        mix_kernel,
        where,
        (
            own,
            other,
            residual.T,
            rows_of(weights, core, 1024, 256),
            rows_of(weights, 1 - core, 1024, 256),
        ),
        [((2, 256, 128), jnp.bfloat16)],
        2 * 256 * 256 * 2048,
        [pltpu.VMEM((256, 256), jnp.float32)],
    )[0]
    spread = jnp.broadcast_to(mixed[:, None], (2, 8, 256, 128)).reshape(16, 256, 128)
    pairs = gather_plane(spread)
    weights = after(weights, pairs)
    pairs = pairs.reshape(2, 8, 256, 128)
    own = (pairs[0].astype(jnp.float32) + pairs[1].astype(jnp.float32)).astype(jnp.bfloat16)
    w_own, w_other = rows_of(weights, core, 0, 1024), rows_of(weights, 1 - core, 0, 1024)
    other = swap(own, "core")
    gains = lax.dynamic_index_in_dim(norm_gain.reshape(8, 2, 2, 128), side, 2, keepdims=False)
    gain_own = lax.dynamic_index_in_dim(gains, core, 1, keepdims=False).reshape(1, 1024)
    gain_other = lax.dynamic_index_in_dim(gains, 1 - core, 1, keepdims=False).reshape(1, 1024)
    begun, power = local_call(
        first_kernel,
        where,
        (own, gain_own, w_own),
        [((256, 1024), jnp.float32), ((256, 128), jnp.float32)],
        2 * 256 * 1024 * 1024,
    )
    other = after(other, begun)
    far = local_call(
        far_kernel,
        where,
        (other, gain_other, begun, power, own, w_other),
        [((160, 1024), jnp.bfloat16)],
        2 * 128 * 1024 * 1024,
    )[0]
    near, power = local_call(
        near_kernel,
        where,
        (other, gain_other, begun, power, w_other),
        [((128, 1024), jnp.float32), ((128, 128), jnp.float32)],
        2 * 128 * 1024 * 1024,
    )
    far = swap(far, "xl")
    far = after(far, near)
    far, hidden, stream = local_call(
        down_far_kernel,
        where,
        (near, far, power, own, w_down),
        [((8, 128, 256), jnp.bfloat16), ((128, 512), jnp.bfloat16), ((128, 256), jnp.bfloat16)],
        2 * 128 * 512 * 2048,
    )
    far = swap(far, "core")
    (near,) = local_call(
        down_near_kernel,
        where,
        (hidden, w_down),
        [((8, 128, 256), jnp.float32)],
        2 * 128 * 512 * 2048,
    )
    far = after(far, near)
    down = (near + far.astype(jnp.float32)).astype(jnp.bfloat16)
    parts = lax.all_to_all(
        down,
        ("y", "xh"),
        split_axis=0,
        concat_axis=0,
        tiled=True,
    )
    down_out = jnp.sum(parts.astype(jnp.float32), axis=0)
    return (stream.astype(jnp.float32) + down_out).astype(jnp.bfloat16).T


def solution(mesh):
    fine = Mesh(mesh.devices.reshape(16, 2, 4, 2, 2), ("z", "xl", "y", "xh", "core"))
    placed = (
        P(COL, ROW),
        P(COL, ROW),
        P(COL, ROW),
        P(COL + ROW, None),
        P(COL + ROW),
        P(COL, ROW),
        P(),
        P(ROW, COL),
        P(ROW, COL),
        P(ROW, COL),
        P(COL, None),
    )
    return jax.shard_map(
        on_device, mesh=fine, in_specs=placed, out_specs=P(COL, ROW), check_vma=False
    )
```

```python
import math

import jax
import jax.numpy as jnp
from jax import lax
from jax.experimental import pallas as pl
from jax.experimental.pallas import tpu as pltpu
from jax.sharding import Mesh
from jax.sharding import PartitionSpec as P

EPSILON = 1e-05
TWO_PI = 2.0 * math.pi
ROW = ("z", "xl")
COL = ("y", "xh", "core")


def dft_tables(length):
    span = 2 * length
    tall = span // 128
    half_rows = length // 128
    k_first = jnp.arange(tall, dtype=jnp.int32)[:, None]
    n_first = jnp.arange(half_rows, dtype=jnp.int32)[None, :]
    angle_first = (k_first * n_first % tall).astype(jnp.float32) * (TWO_PI / tall)
    n_second = jnp.arange(128, dtype=jnp.int32)[None, :]
    angle_twist = (k_first * n_second % span).astype(jnp.float32) * (TWO_PI / span)
    k_second = jnp.arange(128, dtype=jnp.int32)
    angle_second = (k_second[:, None] * k_second[None, :] % 128).astype(jnp.float32) * (
        TWO_PI / 128
    )
    return (
        jnp.cos(angle_first),
        -jnp.sin(angle_first),
        jnp.cos(angle_twist),
        -jnp.sin(angle_twist),
        jnp.cos(angle_second),
        -jnp.sin(angle_second),
    )


def apply_first(matrix, blocks):
    return jnp.einsum("kn,cnm->ckm", matrix, blocks, precision=lax.Precision.HIGHEST)


def apply_last(blocks, matrix):
    return jnp.einsum("ckn,nm->ckm", blocks, matrix, precision=lax.Precision.HIGHEST)


def apply_back(matrix, blocks):
    return jnp.einsum("kn,ckm->cnm", matrix, blocks, precision=lax.Precision.HIGHEST)


def forward_dft(signal, tables):
    cos_first, sin_first, twist_re, twist_im, cos_second, sin_second = tables
    blocks = signal.reshape(signal.shape[0], signal.shape[1] // 128, 128)
    first_re = apply_first(cos_first, blocks)
    first_im = apply_first(sin_first, blocks)
    turned_re = first_re * twist_re - first_im * twist_im
    turned_im = first_re * twist_im + first_im * twist_re
    spec_re = apply_last(turned_re, cos_second) - apply_last(turned_im, sin_second)
    spec_im = apply_last(turned_re, sin_second) + apply_last(turned_im, cos_second)
    return (spec_re, spec_im)


def inverse_dft(spec_re, spec_im, tables, length):
    cos_first, sin_first, twist_re, twist_im, cos_second, sin_second = tables
    back_re = apply_last(spec_re, cos_second) + apply_last(spec_im, sin_second)
    back_im = apply_last(spec_im, cos_second) - apply_last(spec_re, sin_second)
    turned_re = back_re * twist_re + back_im * twist_im
    turned_im = back_im * twist_re - back_re * twist_im
    signal = (apply_back(cos_first, turned_re) + apply_back(sin_first, turned_im)) / (2.0 * length)
    return signal.reshape(signal.shape[0], length)


def swap(array, axis):
    return lax.ppermute(array, axis, [(0, 1), (1, 0)])


def after(array, *others):
    return lax.optimization_barrier((array,) + others)[0]


def gather_plane(spread):
    return lax.all_to_all(spread, ("xl", "y", "xh"), split_axis=0, concat_axis=0, tiled=True)


def mix_kernel(
    where_ref, own_ref, other_ref, residual_ref, w_own_ref, w_other_ref, out_ref, total_ref
):
    total = jnp.zeros((256, 256), jnp.float32)
    for parts_ref, w_ref in ((own_ref, w_own_ref), (other_ref, w_other_ref)):
        for i in range(0, 8, 2):
            rows = [
                jnp.concatenate([parts_ref[i + j], parts_ref[8 + i + j]], axis=0) for j in range(2)
            ]
            total += jnp.dot(
                jnp.concatenate(rows, axis=1),
                w_ref[i : i + 2].reshape(256, 256),
                preferred_element_type=jnp.float32,
            )
    total_ref[...] = total
    near = pl.ds(pl.multiple_of(where_ref[1] * 128, 128), 128)
    total_ref[near] = total_ref[near] + residual_ref[...].astype(jnp.float32)
    out_ref[0] = total_ref[:, :128].astype(jnp.bfloat16)
    out_ref[1] = total_ref[:, 128:].astype(jnp.bfloat16)


def half_ffw(tokens, parts_ref, gain_ref, w_ref):
    total, power = 0.0, 0.0
    for i in range(4):
        wide = jnp.concatenate([parts_ref[2 * i, tokens], parts_ref[2 * i + 1, tokens]], axis=1)
        wide = wide.astype(jnp.float32)
        power += jnp.sum(wide * wide, axis=1, keepdims=True)
        scaled = wide * gain_ref[:, i * 256 : i * 256 + 256]
        total += jnp.dot(
            scaled.astype(jnp.bfloat16),
            w_ref[2 * i : 2 * i + 2].reshape(256, 1024),
            preferred_element_type=jnp.float32,
        )
    return total, jnp.broadcast_to(power, (power.shape[0], 128))


def first_kernel(where_ref, parts_ref, gain_ref, w_ref, total_ref, power_ref):
    total_ref[...], power_ref[...] = half_ffw(pl.ds(0, 256), parts_ref, gain_ref, w_ref)


def far_kernel(
    where_ref, parts_ref, gain_ref, begun_ref, power_ref, own_ref, w_ref, out_ref
):
    far = pl.ds(pl.multiple_of((1 - where_ref[1]) * 128, 128), 128)
    total, power = half_ffw(far, parts_ref, gain_ref, w_ref)
    out_ref[:128] = (total + begun_ref[far]).astype(jnp.bfloat16)
    row = (power + power_ref[far]).T[:16]
    high = row.astype(jnp.bfloat16)
    low = (row - high.astype(jnp.float32)).astype(jnp.bfloat16)
    out_ref[128:144] = jnp.concatenate([high, low] * 4, axis=1)
    stream = own_ref[where_ref[2], far]
    out_ref[144:] = jnp.concatenate([stream[16 * i : 16 * i + 16] for i in range(8)], axis=1)


def near_kernel(
    where_ref, parts_ref, gain_ref, begun_ref, power_ref, w_ref, total_ref, own_power_ref
):
    near = pl.ds(pl.multiple_of(where_ref[1] * 128, 128), 128)
    total, power = half_ffw(near, parts_ref, gain_ref, w_ref)
    total_ref[...] = total + begun_ref[near]
    own_power_ref[...] = power + power_ref[near]


def columns_of(w_ref, index, core):
    return w_ref[:, pl.ds(pl.multiple_of((2 * index + core) * 256, 256), 256)]


def down_far_kernel(
    where_ref, near_ref, far_ref, power_ref, own_ref, w_ref, out_ref, hidden_ref, stream_ref
):
    sums = far_ref[128:144].astype(jnp.float32)
    sums = jnp.broadcast_to(sums[:1, :128] + sums[:1, 128:256], (128, 128)).T
    inverse_rms = lax.rsqrt((power_ref[:, :1] + sums[:, :1]) / 4096 + EPSILON)
    both = (near_ref[...] + far_ref[:128].astype(jnp.float32)) * inverse_rms
    hidden = (jax.nn.silu(both[:, :512]) * both[:, 512:]).astype(jnp.bfloat16)
    hidden_ref[...] = hidden
    for i in range(8):
        out_ref[i] = jnp.dot(
            hidden, columns_of(w_ref, i, 1 - where_ref[0]), preferred_element_type=jnp.float32
        ).astype(jnp.bfloat16)
    side = where_ref[1]
    packed = far_ref[144:]
    back = jnp.concatenate([packed[:, 128 * i : 128 * i + 128] for i in range(8)], axis=0)
    kept = own_ref[where_ref[2], pl.ds(pl.multiple_of(side * 128, 128), 128)]
    stream_ref[:, :128] = jnp.where(side == 0, kept, back)
    stream_ref[:, 128:] = jnp.where(side == 0, back, kept)


def down_near_kernel(where_ref, hidden_ref, w_ref, out_ref):
    for i in range(8):
        out_ref[i] = jnp.dot(
            hidden_ref[...], columns_of(w_ref, i, where_ref[0]), preferred_element_type=jnp.float32
        )


def finish_kernel(where_ref, parts_ref, stream_ref, out_ref):
    total = parts_ref[0].astype(jnp.float32)
    for i in range(1, 8):
        total += parts_ref[i].astype(jnp.float32)
    total += stream_ref[...].astype(jnp.float32)
    out_ref[...] = total.T.astype(jnp.bfloat16)


def local_call(kernel, where, operands, outs, flops, scratch=()):
    outs = [jax.ShapeDtypeStruct(shape, dtype) for shape, dtype in outs]
    return pl.pallas_call(
        kernel,
        in_specs=[pl.BlockSpec(memory_space=pltpu.SMEM)]
        + [pl.BlockSpec(memory_space=pltpu.VMEM)] * len(operands),
        out_specs=[pl.BlockSpec(memory_space=pltpu.VMEM)] * len(outs),
        out_shape=outs,
        scratch_shapes=scratch,
        compiler_params=pltpu.CompilerParams(vmem_limit_bytes=16 * 1024 * 1024),
        cost_estimate=pl.CostEstimate(flops=flops, bytes_accessed=2**21, transcendentals=0),
    )(where, *operands)


def on_device(
    q_stream,
    k_stream,
    v_stream,
    long_filter,
    skip_gain,
    residual,
    norm_gain,
    w_out,
    w_gate,
    w_up,
    w_down,
):
    side = lax.axis_index("xl")
    core = lax.axis_index("core")
    column = lax.axis_index(("y", "xh"))
    where = jnp.stack([core, side, column]).astype(jnp.int32)
    weights = lax.all_gather(
        jnp.concatenate([w_gate, w_up, w_out], axis=1), "z", axis=0, tiled=True
    ).reshape(8, 2, 128, 1280)

    def rows_of(gathered, owner, start, width):
        part = lax.dynamic_slice(gathered, (0, owner, 0, start), (8, 1, 128, width))
        return part.reshape(8, 128, width)

    product = (k_stream.astype(jnp.float32) * v_stream.astype(jnp.float32)).astype(jnp.bfloat16)
    signal = lax.all_to_all(product, ROW, split_axis=0, concat_axis=1, tiled=True)
    length = signal.shape[1]
    tables = dft_tables(length)
    taps = jnp.concatenate([long_filter[:, :1] + skip_gain[:, None], long_filter[:, 1:]], axis=1)
    filter_re, filter_im = forward_dft(taps, tables)
    signal_re, signal_im = forward_dft(signal.astype(jnp.float32), tables)
    joint_re = signal_re * filter_re - signal_im * filter_im
    joint_im = signal_re * filter_im + signal_im * filter_re
    convolved = inverse_dft(joint_re, joint_im, tables, length).astype(jnp.bfloat16)
    convolved = lax.all_to_all(convolved, ROW, split_axis=1, concat_axis=0, tiled=True)
    gated = (q_stream.astype(jnp.float32) * convolved.astype(jnp.float32)).astype(jnp.bfloat16)
    gains = lax.dynamic_index_in_dim(norm_gain.reshape(8, 2, 2, 128), side, 2, keepdims=False)
    gain_own = lax.dynamic_index_in_dim(gains, core, 1, keepdims=False).reshape(1, 1024)
    gain_other = lax.dynamic_index_in_dim(gains, 1 - core, 1, keepdims=False).reshape(1, 1024)
    gated, gain_own, gain_other = lax.optimization_barrier((gated, gain_own, gain_other))
    halves = gated.T.reshape(128, 2, 128).transpose(1, 0, 2)[:, None]
    own = gather_plane(jnp.broadcast_to(halves, (2, 8, 128, 128)).reshape(16, 128, 128))
    other = swap(own, "core")
    mixed = local_call(
        mix_kernel,
        where,
        (
            own,
            other,
            residual.T,
            rows_of(weights, core, 1024, 256),
            rows_of(weights, 1 - core, 1024, 256),
        ),
        [((2, 256, 128), jnp.bfloat16)],
        2 * 256 * 256 * 2048,
        [pltpu.VMEM((256, 256), jnp.float32)],
    )[0]
    spread = jnp.broadcast_to(mixed[:, None], (2, 8, 256, 128)).reshape(16, 256, 128)
    pairs = gather_plane(spread)
    weights = after(weights, pairs)
    pairs = pairs.reshape(2, 8, 256, 128)
    own = (pairs[0].astype(jnp.float32) + pairs[1].astype(jnp.float32)).astype(jnp.bfloat16)
    w_own, w_other = rows_of(weights, core, 0, 1024), rows_of(weights, 1 - core, 0, 1024)
    other = swap(own, "core")
    begun, power = local_call(
        first_kernel,
        where,
        (own, gain_own, w_own),
        [((256, 1024), jnp.float32), ((256, 128), jnp.float32)],
        2 * 256 * 1024 * 1024,
    )
    other = after(other, begun)
    far = local_call(
        far_kernel,
        where,
        (other, gain_other, begun, power, own, w_other),
        [((160, 1024), jnp.bfloat16)],
        2 * 128 * 1024 * 1024,
    )[0]
    near, power = local_call(
        near_kernel,
        where,
        (other, gain_other, begun, power, w_other),
        [((128, 1024), jnp.float32), ((128, 128), jnp.float32)],
        2 * 128 * 1024 * 1024,
    )
    far = swap(far, "xl")
    far = after(far, near)
    far, hidden, stream = local_call(
        down_far_kernel,
        where,
        (near, far, power, own, w_down),
        [((8, 128, 256), jnp.bfloat16), ((128, 512), jnp.bfloat16), ((128, 256), jnp.bfloat16)],
        2 * 128 * 512 * 2048,
    )
    far = swap(far, "core")
    (near,) = local_call(
        down_near_kernel,
        where,
        (hidden, w_down),
        [((8, 128, 256), jnp.float32)],
        2 * 128 * 512 * 2048,
    )
    far = after(far, near)
    down = (near + far.astype(jnp.float32)).astype(jnp.bfloat16)
    parts = lax.all_to_all(
        down,
        ("y", "xh"),
        split_axis=0,
        concat_axis=0,
        tiled=True,
    )
    return local_call(
        finish_kernel, where, (parts, stream), [((256, 128), jnp.bfloat16)], 9 * 128 * 256
    )[0]


def solution(mesh):
    fine = Mesh(mesh.devices.reshape(16, 2, 4, 2, 2), ("z", "xl", "y", "xh", "core"))
    placed = (
        P(COL, ROW),
        P(COL, ROW),
        P(COL, ROW),
        P(COL + ROW, None),
        P(COL + ROW),
        P(COL, ROW),
        P(),
        P(ROW, COL),
        P(ROW, COL),
        P(ROW, COL),
        P(COL, None),
    )
    return jax.shard_map(
        on_device, mesh=fine, in_specs=placed, out_specs=P(COL, ROW), check_vma=False
    )
```

```python
import math

import jax
import jax.numpy as jnp
from jax import lax
from jax.experimental import pallas as pl
from jax.experimental.pallas import tpu as pltpu
from jax.sharding import Mesh
from jax.sharding import PartitionSpec as P

EPSILON = 1e-05
TWO_PI = 2.0 * math.pi
ROW = ("z", "xl")
COL = ("y", "xh", "core")


def dft_tables(length):
    span = 2 * length
    tall = span // 128
    half_rows = length // 128
    k_first = jnp.arange(tall, dtype=jnp.int32)[:, None]
    n_first = jnp.arange(half_rows, dtype=jnp.int32)[None, :]
    angle_first = (k_first * n_first % tall).astype(jnp.float32) * (TWO_PI / tall)
    n_second = jnp.arange(128, dtype=jnp.int32)[None, :]
    angle_twist = (k_first * n_second % span).astype(jnp.float32) * (TWO_PI / span)
    k_second = jnp.arange(128, dtype=jnp.int32)
    angle_second = (k_second[:, None] * k_second[None, :] % 128).astype(jnp.float32) * (
        TWO_PI / 128
    )
    return (
        jnp.cos(angle_first),
        -jnp.sin(angle_first),
        jnp.cos(angle_twist),
        -jnp.sin(angle_twist),
        jnp.cos(angle_second),
        -jnp.sin(angle_second),
    )


def apply_first(matrix, blocks):
    return jnp.einsum("kn,cnm->ckm", matrix, blocks, precision=lax.Precision.HIGHEST)


def apply_last(blocks, matrix):
    return jnp.einsum("ckn,nm->ckm", blocks, matrix, precision=lax.Precision.HIGHEST)


def apply_back(matrix, blocks):
    return jnp.einsum("kn,ckm->cnm", matrix, blocks, precision=lax.Precision.HIGHEST)


def forward_dft(signal, tables):
    cos_first, sin_first, twist_re, twist_im, cos_second, sin_second = tables
    blocks = signal.reshape(signal.shape[0], signal.shape[1] // 128, 128)
    first_re = apply_first(cos_first, blocks)
    first_im = apply_first(sin_first, blocks)
    turned_re = first_re * twist_re - first_im * twist_im
    turned_im = first_re * twist_im + first_im * twist_re
    spec_re = apply_last(turned_re, cos_second) - apply_last(turned_im, sin_second)
    spec_im = apply_last(turned_re, sin_second) + apply_last(turned_im, cos_second)
    return (spec_re, spec_im)


def inverse_dft(spec_re, spec_im, tables, length):
    cos_first, sin_first, twist_re, twist_im, cos_second, sin_second = tables
    back_re = apply_last(spec_re, cos_second) + apply_last(spec_im, sin_second)
    back_im = apply_last(spec_im, cos_second) - apply_last(spec_re, sin_second)
    turned_re = back_re * twist_re + back_im * twist_im
    turned_im = back_im * twist_re - back_re * twist_im
    signal = (apply_back(cos_first, turned_re) + apply_back(sin_first, turned_im)) / (2.0 * length)
    return signal.reshape(signal.shape[0], length)


def swap(array, axis):
    return lax.ppermute(array, axis, [(0, 1), (1, 0)])


def after(array, *others):
    return lax.optimization_barrier((array,) + others)[0]


def gather_plane(spread):
    return lax.all_to_all(spread, ("xl", "y", "xh"), split_axis=0, concat_axis=0, tiled=True)


def mix_kernel(
    where_ref, own_ref, other_ref, residual_ref, w_own_ref, w_other_ref, out_ref, total_ref
):
    total = jnp.zeros((256, 256), jnp.float32)
    for parts_ref, w_ref in ((own_ref, w_own_ref), (other_ref, w_other_ref)):
        for i in range(0, 8, 2):
            rows = [
                jnp.concatenate([parts_ref[i + j], parts_ref[8 + i + j]], axis=0) for j in range(2)
            ]
            total += jnp.dot(
                jnp.concatenate(rows, axis=1),
                w_ref[i : i + 2].reshape(256, 256),
                preferred_element_type=jnp.float32,
            )
    total_ref[...] = total
    near = pl.ds(pl.multiple_of(where_ref[1] * 128, 128), 128)
    total_ref[near] = total_ref[near] + residual_ref[...].astype(jnp.float32)
    out_ref[0] = total_ref[:, :128].astype(jnp.bfloat16)
    out_ref[1] = total_ref[:, 128:].astype(jnp.bfloat16)


def half_ffw(tokens, owner, parts_ref, gain_ref, w_ref):
    total, power = 0.0, 0.0
    for i in range(4):
        wide = jnp.concatenate([parts_ref[2 * i, tokens], parts_ref[2 * i + 1, tokens]], axis=1)
        wide = wide.astype(jnp.float32)
        power += jnp.sum(wide * wide, axis=1, keepdims=True)
        scaled = wide * gain_ref[:, i * 256 : i * 256 + 256]
        total += jnp.dot(
            scaled.astype(jnp.bfloat16),
            w_ref[2 * i : 2 * i + 2, owner, :, :1024].reshape(256, 1024),
            preferred_element_type=jnp.float32,
        )
    return total, jnp.broadcast_to(power, (power.shape[0], 128))


def first_kernel(where_ref, parts_ref, gain_ref, w_ref, total_ref, power_ref):
    total_ref[...], power_ref[...] = half_ffw(
        pl.ds(0, 256), where_ref[0], parts_ref, gain_ref, w_ref
    )


def far_kernel(
    where_ref, parts_ref, gain_ref, begun_ref, power_ref, own_ref, w_ref, out_ref
):
    far = pl.ds(pl.multiple_of((1 - where_ref[1]) * 128, 128), 128)
    total, power = half_ffw(far, 1 - where_ref[0], parts_ref, gain_ref, w_ref)
    out_ref[:128] = (total + begun_ref[far]).astype(jnp.bfloat16)
    row = (power + power_ref[far]).T[:16]
    high = row.astype(jnp.bfloat16)
    low = (row - high.astype(jnp.float32)).astype(jnp.bfloat16)
    out_ref[128:144] = jnp.concatenate([high, low] * 4, axis=1)
    stream = own_ref[where_ref[2], far]
    out_ref[144:] = jnp.concatenate([stream[16 * i : 16 * i + 16] for i in range(8)], axis=1)


def near_kernel(
    where_ref, parts_ref, gain_ref, begun_ref, power_ref, w_ref, total_ref, own_power_ref
):
    near = pl.ds(pl.multiple_of(where_ref[1] * 128, 128), 128)
    total, power = half_ffw(near, 1 - where_ref[0], parts_ref, gain_ref, w_ref)
    total_ref[...] = total + begun_ref[near]
    own_power_ref[...] = power + power_ref[near]


def columns_of(w_ref, index, core):
    return w_ref[:, pl.ds(pl.multiple_of((2 * index + core) * 256, 256), 256)]


def down_far_kernel(
    where_ref, near_ref, far_ref, power_ref, own_ref, w_ref, out_ref, hidden_ref, stream_ref
):
    sums = far_ref[128:144].astype(jnp.float32)
    sums = jnp.broadcast_to(sums[:1, :128] + sums[:1, 128:256], (128, 128)).T
    inverse_rms = lax.rsqrt((power_ref[:, :1] + sums[:, :1]) / 4096 + EPSILON)
    both = (near_ref[...] + far_ref[:128].astype(jnp.float32)) * inverse_rms
    hidden = (jax.nn.silu(both[:, :512]) * both[:, 512:]).astype(jnp.bfloat16)
    hidden_ref[...] = hidden
    for i in range(8):
        out_ref[i] = jnp.dot(
            hidden, columns_of(w_ref, i, 1 - where_ref[0]), preferred_element_type=jnp.float32
        ).astype(jnp.bfloat16)
    side = where_ref[1]
    packed = far_ref[144:]
    back = jnp.concatenate([packed[:, 128 * i : 128 * i + 128] for i in range(8)], axis=0)
    kept = own_ref[where_ref[2], pl.ds(pl.multiple_of(side * 128, 128), 128)]
    stream_ref[:, :128] = jnp.where(side == 0, kept, back)
    stream_ref[:, 128:] = jnp.where(side == 0, back, kept)


def down_near_kernel(where_ref, hidden_ref, w_ref, out_ref):
    for i in range(8):
        out_ref[i] = jnp.dot(
            hidden_ref[...], columns_of(w_ref, i, where_ref[0]), preferred_element_type=jnp.float32
        )


def local_call(kernel, where, operands, outs, flops, scratch=()):
    outs = [jax.ShapeDtypeStruct(shape, dtype) for shape, dtype in outs]
    return pl.pallas_call(
        kernel,
        in_specs=[pl.BlockSpec(memory_space=pltpu.SMEM)]
        + [pl.BlockSpec(memory_space=pltpu.VMEM)] * len(operands),
        out_specs=[pl.BlockSpec(memory_space=pltpu.VMEM)] * len(outs),
        out_shape=outs,
        scratch_shapes=scratch,
        compiler_params=pltpu.CompilerParams(vmem_limit_bytes=16 * 1024 * 1024),
        cost_estimate=pl.CostEstimate(flops=flops, bytes_accessed=2**21, transcendentals=0),
    )(where, *operands)


def on_device(
    q_stream,
    k_stream,
    v_stream,
    long_filter,
    skip_gain,
    residual,
    norm_gain,
    w_out,
    w_gate,
    w_up,
    w_down,
):
    side = lax.axis_index("xl")
    core = lax.axis_index("core")
    column = lax.axis_index(("y", "xh"))
    where = jnp.stack([core, side, column]).astype(jnp.int32)
    weights = lax.all_gather(
        jnp.concatenate([w_gate, w_up, w_out], axis=1), "z", axis=0, tiled=True
    ).reshape(8, 2, 128, 1280)

    def rows_of(gathered, owner, start, width):
        part = lax.dynamic_slice(gathered, (0, owner, 0, start), (8, 1, 128, width))
        return part.reshape(8, 128, width)

    product = (k_stream.astype(jnp.float32) * v_stream.astype(jnp.float32)).astype(jnp.bfloat16)
    signal = lax.all_to_all(product, ROW, split_axis=0, concat_axis=1, tiled=True)
    length = signal.shape[1]
    tables = dft_tables(length)
    taps = jnp.concatenate([long_filter[:, :1] + skip_gain[:, None], long_filter[:, 1:]], axis=1)
    filter_re, filter_im = forward_dft(taps, tables)
    signal_re, signal_im = forward_dft(signal.astype(jnp.float32), tables)
    joint_re = signal_re * filter_re - signal_im * filter_im
    joint_im = signal_re * filter_im + signal_im * filter_re
    convolved = inverse_dft(joint_re, joint_im, tables, length).astype(jnp.bfloat16)
    convolved = lax.all_to_all(convolved, ROW, split_axis=1, concat_axis=0, tiled=True)
    gated = (q_stream.astype(jnp.float32) * convolved.astype(jnp.float32)).astype(jnp.bfloat16)
    gains = lax.dynamic_index_in_dim(norm_gain.reshape(8, 2, 2, 128), side, 2, keepdims=False)
    gain_own = lax.dynamic_index_in_dim(gains, core, 1, keepdims=False).reshape(1, 1024)
    gain_other = lax.dynamic_index_in_dim(gains, 1 - core, 1, keepdims=False).reshape(1, 1024)
    gated, gain_own, gain_other = lax.optimization_barrier((gated, gain_own, gain_other))
    halves = gated.T.reshape(128, 2, 128).transpose(1, 0, 2)[:, None]
    own = gather_plane(jnp.broadcast_to(halves, (2, 8, 128, 128)).reshape(16, 128, 128))
    other = swap(own, "core")
    mixed = local_call(
        mix_kernel,
        where,
        (
            own,
            other,
            residual.T,
            rows_of(weights, core, 1024, 256),
            rows_of(weights, 1 - core, 1024, 256),
        ),
        [((2, 256, 128), jnp.bfloat16)],
        2 * 256 * 256 * 2048,
        [pltpu.VMEM((256, 256), jnp.float32)],
    )[0]
    spread = jnp.broadcast_to(mixed[:, None], (2, 8, 256, 128)).reshape(16, 256, 128)
    pairs = gather_plane(spread)
    weights = after(weights, pairs)
    pairs = pairs.reshape(2, 8, 256, 128)
    own = (pairs[0].astype(jnp.float32) + pairs[1].astype(jnp.float32)).astype(jnp.bfloat16)
    other = swap(own, "core")
    begun, power = local_call(
        first_kernel,
        where,
        (own, gain_own, weights),
        [((256, 1024), jnp.float32), ((256, 128), jnp.float32)],
        2 * 256 * 1024 * 1024,
    )
    other = after(other, begun)
    far = local_call(
        far_kernel,
        where,
        (other, gain_other, begun, power, own, weights),
        [((160, 1024), jnp.bfloat16)],
        2 * 128 * 1024 * 1024,
    )[0]
    near, power = local_call(
        near_kernel,
        where,
        (other, gain_other, begun, power, weights),
        [((128, 1024), jnp.float32), ((128, 128), jnp.float32)],
        2 * 128 * 1024 * 1024,
    )
    far = swap(far, "xl")
    far = after(far, near)
    far, hidden, stream = local_call(
        down_far_kernel,
        where,
        (near, far, power, own, w_down),
        [((8, 128, 256), jnp.bfloat16), ((128, 512), jnp.bfloat16), ((128, 256), jnp.bfloat16)],
        2 * 128 * 512 * 2048,
    )
    far = swap(far, "core")
    (near,) = local_call(
        down_near_kernel,
        where,
        (hidden, w_down),
        [((8, 128, 256), jnp.float32)],
        2 * 128 * 512 * 2048,
    )
    far = after(far, near)
    down = (near + far.astype(jnp.float32)).astype(jnp.bfloat16)
    parts = lax.all_to_all(
        down,
        ("y", "xh"),
        split_axis=0,
        concat_axis=0,
        tiled=True,
    )
    down_out = jnp.sum(parts.astype(jnp.float32), axis=0)
    return (stream.astype(jnp.float32) + down_out).astype(jnp.bfloat16).T


def solution(mesh):
    fine = Mesh(mesh.devices.reshape(16, 2, 4, 2, 2), ("z", "xl", "y", "xh", "core"))
    placed = (
        P(COL, ROW),
        P(COL, ROW),
        P(COL, ROW),
        P(COL + ROW, None),
        P(COL + ROW),
        P(COL, ROW),
        P(),
        P(ROW, COL),
        P(ROW, COL),
        P(ROW, COL),
        P(COL, None),
    )
    return jax.shard_map(
        on_device, mesh=fine, in_specs=placed, out_specs=P(COL, ROW), check_vma=False
    )
```

```python
import math

import jax
import jax.numpy as jnp
from jax import lax
from jax.experimental import pallas as pl
from jax.experimental.pallas import tpu as pltpu
from jax.sharding import Mesh
from jax.sharding import PartitionSpec as P

EPSILON = 1e-05
TWO_PI = 2.0 * math.pi
ROW = ("z", "xl")
COL = ("y", "xh", "core")


def dft_tables(length):
    span = 2 * length
    tall = span // 128
    half_rows = length // 128
    k_first = jnp.arange(tall, dtype=jnp.int32)[:, None]
    n_first = jnp.arange(half_rows, dtype=jnp.int32)[None, :]
    angle_first = (k_first * n_first % tall).astype(jnp.float32) * (TWO_PI / tall)
    n_second = jnp.arange(128, dtype=jnp.int32)[None, :]
    angle_twist = (k_first * n_second % span).astype(jnp.float32) * (TWO_PI / span)
    k_second = jnp.arange(128, dtype=jnp.int32)
    angle_second = (k_second[:, None] * k_second[None, :] % 128).astype(jnp.float32) * (
        TWO_PI / 128
    )
    return (
        jnp.cos(angle_first),
        -jnp.sin(angle_first),
        jnp.cos(angle_twist),
        -jnp.sin(angle_twist),
        jnp.cos(angle_second),
        -jnp.sin(angle_second),
    )


def apply_first(matrix, blocks):
    return jnp.einsum("kn,cnm->ckm", matrix, blocks, precision=lax.Precision.HIGHEST)


def apply_last(blocks, matrix):
    return jnp.einsum("ckn,nm->ckm", blocks, matrix, precision=lax.Precision.HIGHEST)


def apply_back(matrix, blocks):
    return jnp.einsum("kn,ckm->cnm", matrix, blocks, precision=lax.Precision.HIGHEST)


def forward_dft(signal, tables):
    cos_first, sin_first, twist_re, twist_im, cos_second, sin_second = tables
    blocks = signal.reshape(signal.shape[0], signal.shape[1] // 128, 128)
    first_re = apply_first(cos_first, blocks)
    first_im = apply_first(sin_first, blocks)
    turned_re = first_re * twist_re - first_im * twist_im
    turned_im = first_re * twist_im + first_im * twist_re
    spec_re = apply_last(turned_re, cos_second) - apply_last(turned_im, sin_second)
    spec_im = apply_last(turned_re, sin_second) + apply_last(turned_im, cos_second)
    return (spec_re, spec_im)


def inverse_dft(spec_re, spec_im, tables, length):
    cos_first, sin_first, twist_re, twist_im, cos_second, sin_second = tables
    back_re = apply_last(spec_re, cos_second) + apply_last(spec_im, sin_second)
    back_im = apply_last(spec_im, cos_second) - apply_last(spec_re, sin_second)
    turned_re = back_re * twist_re + back_im * twist_im
    turned_im = back_im * twist_re - back_re * twist_im
    signal = (apply_back(cos_first, turned_re) + apply_back(sin_first, turned_im)) / (2.0 * length)
    return signal.reshape(signal.shape[0], length)


def swap(array, axis):
    return lax.ppermute(array, axis, [(0, 1), (1, 0)])


def after(array, *others):
    return lax.optimization_barrier((array,) + others)[0]


def gather_plane(spread):
    return lax.all_to_all(spread, ("xl", "y", "xh"), split_axis=0, concat_axis=0, tiled=True)


def mix_kernel(
    where_ref, own_ref, other_ref, residual_ref, w_own_ref, w_other_ref, out_ref, total_ref
):
    total = jnp.zeros((256, 256), jnp.float32)
    for parts_ref, w_ref in ((own_ref, w_own_ref), (other_ref, w_other_ref)):
        for i in range(0, 8, 2):
            rows = [
                jnp.concatenate([parts_ref[i + j], parts_ref[8 + i + j]], axis=0) for j in range(2)
            ]
            total += jnp.dot(
                jnp.concatenate(rows, axis=1),
                w_ref[i : i + 2].reshape(256, 256),
                preferred_element_type=jnp.float32,
            )
    total_ref[...] = total
    near = pl.ds(pl.multiple_of(where_ref[1] * 128, 128), 128)
    total_ref[near] = total_ref[near] + residual_ref[...].astype(jnp.float32)
    out_ref[0] = total_ref[:, :128].astype(jnp.bfloat16)
    out_ref[1] = total_ref[:, 128:].astype(jnp.bfloat16)


def half_ffw(tokens, owner, parts_ref, gain_ref, w_ref):
    total, power = 0.0, 0.0
    for i in range(4):
        wide = jnp.concatenate([parts_ref[2 * i, tokens], parts_ref[2 * i + 1, tokens]], axis=1)
        wide = wide.astype(jnp.float32)
        power += jnp.sum(wide * wide, axis=1, keepdims=True)
        scaled = wide * gain_ref[:, i * 256 : i * 256 + 256]
        total += jnp.dot(
            scaled.astype(jnp.bfloat16),
            w_ref[2 * i : 2 * i + 2, owner, :, :1024].reshape(256, 1024),
            preferred_element_type=jnp.float32,
        )
    return total, jnp.broadcast_to(power, (power.shape[0], 128))


def first_kernel(where_ref, parts_ref, gain_ref, w_ref, total_ref, power_ref):
    total_ref[...], power_ref[...] = half_ffw(
        pl.ds(0, 256), where_ref[0], parts_ref, gain_ref, w_ref
    )


def far_kernel(
    where_ref, parts_ref, gain_ref, begun_ref, power_ref, own_ref, w_ref, out_ref
):
    far = pl.ds(pl.multiple_of((1 - where_ref[1]) * 128, 128), 128)
    total, power = half_ffw(far, 1 - where_ref[0], parts_ref, gain_ref, w_ref)
    out_ref[:128] = (total + begun_ref[far]).astype(jnp.bfloat16)
    row = (power + power_ref[far]).T[:16]
    high = row.astype(jnp.bfloat16)
    low = (row - high.astype(jnp.float32)).astype(jnp.bfloat16)
    out_ref[128:144] = jnp.concatenate([high, low] * 4, axis=1)
    stream = own_ref[where_ref[2], far]
    out_ref[144:] = jnp.concatenate([stream[16 * i : 16 * i + 16] for i in range(8)], axis=1)


def near_kernel(
    where_ref, parts_ref, gain_ref, begun_ref, power_ref, w_ref, total_ref, own_power_ref
):
    near = pl.ds(pl.multiple_of(where_ref[1] * 128, 128), 128)
    total, power = half_ffw(near, 1 - where_ref[0], parts_ref, gain_ref, w_ref)
    total_ref[...] = total + begun_ref[near]
    own_power_ref[...] = power + power_ref[near]


def columns_of(w_ref, index, core):
    column = 2 * (index % 4) + index // 4
    return w_ref[:, pl.ds(pl.multiple_of((2 * column + core) * 256, 256), 256)]


def down_far_kernel(
    where_ref, near_ref, far_ref, power_ref, own_ref, w_ref, out_ref, hidden_ref, stream_ref
):
    sums = far_ref[128:144].astype(jnp.float32)
    sums = jnp.broadcast_to(sums[:1, :128] + sums[:1, 128:256], (128, 128)).T
    inverse_rms = lax.rsqrt((power_ref[:, :1] + sums[:, :1]) / 4096 + EPSILON)
    both = (near_ref[...] + far_ref[:128].astype(jnp.float32)) * inverse_rms
    hidden = (jax.nn.silu(both[:, :512]) * both[:, 512:]).astype(jnp.bfloat16)
    hidden_ref[...] = hidden
    for i in range(8):
        out_ref[i] = jnp.dot(
            hidden, columns_of(w_ref, i, 1 - where_ref[0]), preferred_element_type=jnp.float32
        ).astype(jnp.bfloat16)
    side = where_ref[1]
    packed = far_ref[144:]
    back = jnp.concatenate([packed[:, 128 * i : 128 * i + 128] for i in range(8)], axis=0)
    kept = own_ref[where_ref[2], pl.ds(pl.multiple_of(side * 128, 128), 128)]
    stream_ref[:, :128] = jnp.where(side == 0, kept, back)
    stream_ref[:, 128:] = jnp.where(side == 0, back, kept)


def down_near_kernel(where_ref, hidden_ref, w_ref, out_ref):
    for i in range(8):
        out_ref[i] = jnp.dot(
            hidden_ref[...], columns_of(w_ref, i, where_ref[0]), preferred_element_type=jnp.float32
        )


def local_call(kernel, where, operands, outs, flops, scratch=()):
    outs = [jax.ShapeDtypeStruct(shape, dtype) for shape, dtype in outs]
    return pl.pallas_call(
        kernel,
        in_specs=[pl.BlockSpec(memory_space=pltpu.SMEM)]
        + [pl.BlockSpec(memory_space=pltpu.VMEM)] * len(operands),
        out_specs=[pl.BlockSpec(memory_space=pltpu.VMEM)] * len(outs),
        out_shape=outs,
        scratch_shapes=scratch,
        compiler_params=pltpu.CompilerParams(vmem_limit_bytes=16 * 1024 * 1024),
        cost_estimate=pl.CostEstimate(flops=flops, bytes_accessed=2**21, transcendentals=0),
    )(where, *operands)


def on_device(
    q_stream,
    k_stream,
    v_stream,
    long_filter,
    skip_gain,
    residual,
    norm_gain,
    w_out,
    w_gate,
    w_up,
    w_down,
):
    side = lax.axis_index("xl")
    core = lax.axis_index("core")
    column = lax.axis_index(("y", "xh"))
    where = jnp.stack([core, side, column]).astype(jnp.int32)
    weights = lax.all_gather(
        jnp.concatenate([w_gate, w_up, w_out], axis=1), "z", axis=0, tiled=True
    ).reshape(8, 2, 128, 1280)

    def rows_of(gathered, owner, start, width):
        part = lax.dynamic_slice(gathered, (0, owner, 0, start), (8, 1, 128, width))
        return part.reshape(8, 128, width)

    product = (k_stream.astype(jnp.float32) * v_stream.astype(jnp.float32)).astype(jnp.bfloat16)
    signal = lax.all_to_all(product, ROW, split_axis=0, concat_axis=1, tiled=True)
    length = signal.shape[1]
    tables = dft_tables(length)
    taps = jnp.concatenate([long_filter[:, :1] + skip_gain[:, None], long_filter[:, 1:]], axis=1)
    filter_re, filter_im = forward_dft(taps, tables)
    signal_re, signal_im = forward_dft(signal.astype(jnp.float32), tables)
    joint_re = signal_re * filter_re - signal_im * filter_im
    joint_im = signal_re * filter_im + signal_im * filter_re
    convolved = inverse_dft(joint_re, joint_im, tables, length).astype(jnp.bfloat16)
    convolved = lax.all_to_all(convolved, ROW, split_axis=1, concat_axis=0, tiled=True)
    gated = (q_stream.astype(jnp.float32) * convolved.astype(jnp.float32)).astype(jnp.bfloat16)
    gains = lax.dynamic_index_in_dim(norm_gain.reshape(8, 2, 2, 128), side, 2, keepdims=False)
    gain_own = lax.dynamic_index_in_dim(gains, core, 1, keepdims=False).reshape(1, 1024)
    gain_other = lax.dynamic_index_in_dim(gains, 1 - core, 1, keepdims=False).reshape(1, 1024)
    gated, gain_own, gain_other = lax.optimization_barrier((gated, gain_own, gain_other))
    halves = gated.T.reshape(128, 2, 128).transpose(1, 0, 2)[:, None]
    own = gather_plane(jnp.broadcast_to(halves, (2, 8, 128, 128)).reshape(16, 128, 128))
    other = swap(own, "core")
    mixed = local_call(
        mix_kernel,
        where,
        (
            own,
            other,
            residual.T,
            rows_of(weights, core, 1024, 256),
            rows_of(weights, 1 - core, 1024, 256),
        ),
        [((2, 256, 128), jnp.bfloat16)],
        2 * 256 * 256 * 2048,
        [pltpu.VMEM((256, 256), jnp.float32)],
    )[0]
    spread = jnp.broadcast_to(mixed[None, :, None], (4, 2, 2, 256, 128)).reshape(16, 256, 128)
    pairs = lax.all_to_all(spread, ("y", "xl", "xh"), split_axis=0, concat_axis=0, tiled=True)
    weights = after(weights, pairs)
    pairs = pairs.reshape(4, 2, 2, 256, 128)
    own = (pairs[:, 0].astype(jnp.float32) + pairs[:, 1].astype(jnp.float32)).astype(jnp.bfloat16)
    own = own.reshape(8, 256, 128)
    other = swap(own, "core")
    begun, power = local_call(
        first_kernel,
        where,
        (own, gain_own, weights),
        [((256, 1024), jnp.float32), ((256, 128), jnp.float32)],
        2 * 256 * 1024 * 1024,
    )
    other = after(other, begun)
    far = local_call(
        far_kernel,
        where,
        (other, gain_other, begun, power, own, weights),
        [((160, 1024), jnp.bfloat16)],
        2 * 128 * 1024 * 1024,
    )[0]
    near, power = local_call(
        near_kernel,
        where,
        (other, gain_other, begun, power, weights),
        [((128, 1024), jnp.float32), ((128, 128), jnp.float32)],
        2 * 128 * 1024 * 1024,
    )
    far = swap(far, "xl")
    far = after(far, near)
    far, hidden, stream = local_call(
        down_far_kernel,
        where,
        (near, far, power, own, w_down),
        [((8, 128, 256), jnp.bfloat16), ((128, 512), jnp.bfloat16), ((128, 256), jnp.bfloat16)],
        2 * 128 * 512 * 2048,
    )
    far = swap(far, "core")
    (near,) = local_call(
        down_near_kernel,
        where,
        (hidden, w_down),
        [((8, 128, 256), jnp.float32)],
        2 * 128 * 512 * 2048,
    )
    far = after(far, near)
    down = (near + far.astype(jnp.float32)).astype(jnp.bfloat16)
    parts = lax.all_to_all(
        down,
        ("xh", "y"),
        split_axis=0,
        concat_axis=0,
        tiled=True,
    )
    down_out = jnp.sum(parts.astype(jnp.float32), axis=0)
    return (stream.astype(jnp.float32) + down_out).astype(jnp.bfloat16).T


def solution(mesh):
    fine = Mesh(mesh.devices.reshape(16, 2, 4, 2, 2), ("z", "xl", "y", "xh", "core"))
    placed = (
        P(COL, ROW),
        P(COL, ROW),
        P(COL, ROW),
        P(COL + ROW, None),
        P(COL + ROW),
        P(COL, ROW),
        P(),
        P(ROW, COL),
        P(ROW, COL),
        P(ROW, COL),
        P(COL, None),
    )
    return jax.shard_map(
        on_device, mesh=fine, in_specs=placed, out_specs=P(COL, ROW), check_vma=False
    )
```

```python
import math

import jax
import jax.numpy as jnp
from jax import lax
from jax.experimental import pallas as pl
from jax.experimental.pallas import tpu as pltpu
from jax.sharding import Mesh
from jax.sharding import PartitionSpec as P

EPSILON = 1e-05
TWO_PI = 2.0 * math.pi
ROW = ("z", "xl")
COL = ("y", "xh", "core")


def dft_tables(length):
    span = 2 * length
    tall = span // 128
    half_rows = length // 128
    k_first = jnp.arange(tall, dtype=jnp.int32)[:, None]
    n_first = jnp.arange(half_rows, dtype=jnp.int32)[None, :]
    angle_first = (k_first * n_first % tall).astype(jnp.float32) * (TWO_PI / tall)
    n_second = jnp.arange(128, dtype=jnp.int32)[None, :]
    angle_twist = (k_first * n_second % span).astype(jnp.float32) * (TWO_PI / span)
    k_second = jnp.arange(128, dtype=jnp.int32)
    angle_second = (k_second[:, None] * k_second[None, :] % 128).astype(jnp.float32) * (
        TWO_PI / 128
    )
    return (
        jnp.cos(angle_first),
        -jnp.sin(angle_first),
        jnp.cos(angle_twist),
        -jnp.sin(angle_twist),
        jnp.cos(angle_second),
        -jnp.sin(angle_second),
    )


def apply_first(matrix, blocks):
    return jnp.einsum("kn,cnm->ckm", matrix, blocks, precision=lax.Precision.HIGHEST)


def apply_last(blocks, matrix):
    return jnp.einsum("ckn,nm->ckm", blocks, matrix, precision=lax.Precision.HIGHEST)


def apply_back(matrix, blocks):
    return jnp.einsum("kn,ckm->cnm", matrix, blocks, precision=lax.Precision.HIGHEST)


def forward_dft(signal, tables):
    cos_first, sin_first, twist_re, twist_im, cos_second, sin_second = tables
    blocks = signal.reshape(signal.shape[0], signal.shape[1] // 128, 128)
    first_re = apply_first(cos_first, blocks)
    first_im = apply_first(sin_first, blocks)
    turned_re = first_re * twist_re - first_im * twist_im
    turned_im = first_re * twist_im + first_im * twist_re
    spec_re = apply_last(turned_re, cos_second) - apply_last(turned_im, sin_second)
    spec_im = apply_last(turned_re, sin_second) + apply_last(turned_im, cos_second)
    return (spec_re, spec_im)


def inverse_dft(spec_re, spec_im, tables, length):
    cos_first, sin_first, twist_re, twist_im, cos_second, sin_second = tables
    back_re = apply_last(spec_re, cos_second) + apply_last(spec_im, sin_second)
    back_im = apply_last(spec_im, cos_second) - apply_last(spec_re, sin_second)
    turned_re = back_re * twist_re + back_im * twist_im
    turned_im = back_im * twist_re - back_re * twist_im
    signal = (apply_back(cos_first, turned_re) + apply_back(sin_first, turned_im)) / (2.0 * length)
    return signal.reshape(signal.shape[0], length)


def swap(array, axis):
    return lax.ppermute(array, axis, [(0, 1), (1, 0)])


def after(array, *others):
    return lax.optimization_barrier((array,) + others)[0]


def gather_plane(spread):
    return lax.all_to_all(spread, ("xl", "y", "xh"), split_axis=0, concat_axis=0, tiled=True)


def mix_kernel(
    where_ref, own_ref, other_ref, residual_ref, w_ref, out_ref, total_ref
):
    total = jnp.zeros((256, 256), jnp.float32)
    core = where_ref[0]
    for parts_ref, owner in ((own_ref, core), (other_ref, 1 - core)):
        for i in range(0, 8, 2):
            rows = [
                jnp.concatenate([parts_ref[i + j], parts_ref[8 + i + j]], axis=0) for j in range(2)
            ]
            total += jnp.dot(
                jnp.concatenate(rows, axis=1),
                w_ref[i : i + 2, owner].reshape(256, 256),
                preferred_element_type=jnp.float32,
            )
    total_ref[...] = total
    near = pl.ds(pl.multiple_of(where_ref[1] * 128, 128), 128)
    total_ref[near] = total_ref[near] + residual_ref[...].astype(jnp.float32)
    out_ref[0] = total_ref[:, :128].astype(jnp.bfloat16)
    out_ref[1] = total_ref[:, 128:].astype(jnp.bfloat16)


def half_ffw(tokens, owner, parts_ref, gain_ref, w_ref):
    total, power = 0.0, 0.0
    for i in range(4):
        wide = jnp.concatenate([parts_ref[2 * i, tokens], parts_ref[2 * i + 1, tokens]], axis=1)
        wide = wide.astype(jnp.float32)
        power += jnp.sum(wide * wide, axis=1, keepdims=True)
        scaled = wide * gain_ref[:, i * 256 : i * 256 + 256]
        total += jnp.dot(
            scaled.astype(jnp.bfloat16),
            w_ref[2 * i : 2 * i + 2, owner, :, :1024].reshape(256, 1024),
            preferred_element_type=jnp.float32,
        )
    return total, jnp.broadcast_to(power, (power.shape[0], 128))


def first_kernel(where_ref, parts_ref, gain_ref, w_ref, total_ref, power_ref):
    total_ref[...], power_ref[...] = half_ffw(
        pl.ds(0, 256), where_ref[0], parts_ref, gain_ref, w_ref
    )


def far_kernel(
    where_ref, parts_ref, gain_ref, begun_ref, power_ref, own_ref, w_ref, out_ref
):
    far = pl.ds(pl.multiple_of((1 - where_ref[1]) * 128, 128), 128)
    total, power = half_ffw(far, 1 - where_ref[0], parts_ref, gain_ref, w_ref)
    out_ref[:128] = (total + begun_ref[far]).astype(jnp.bfloat16)
    row = (power + power_ref[far]).T[:16]
    high = row.astype(jnp.bfloat16)
    low = (row - high.astype(jnp.float32)).astype(jnp.bfloat16)
    out_ref[128:144] = jnp.concatenate([high, low] * 4, axis=1)
    stream = own_ref[where_ref[2], far]
    out_ref[144:] = jnp.concatenate([stream[16 * i : 16 * i + 16] for i in range(8)], axis=1)


def near_kernel(
    where_ref, parts_ref, gain_ref, begun_ref, power_ref, w_ref, total_ref, own_power_ref
):
    near = pl.ds(pl.multiple_of(where_ref[1] * 128, 128), 128)
    total, power = half_ffw(near, 1 - where_ref[0], parts_ref, gain_ref, w_ref)
    total_ref[...] = total + begun_ref[near]
    own_power_ref[...] = power + power_ref[near]


def columns_of(w_ref, index, core):
    column = 2 * (index % 4) + index // 4
    return w_ref[:, pl.ds(pl.multiple_of((2 * column + core) * 256, 256), 256)]


def down_far_kernel(
    where_ref, near_ref, far_ref, power_ref, own_ref, w_ref, out_ref, hidden_ref, stream_ref
):
    sums = far_ref[128:144].astype(jnp.float32)
    sums = jnp.broadcast_to(sums[:1, :128] + sums[:1, 128:256], (128, 128)).T
    inverse_rms = lax.rsqrt((power_ref[:, :1] + sums[:, :1]) / 4096 + EPSILON)
    both = (near_ref[...] + far_ref[:128].astype(jnp.float32)) * inverse_rms
    hidden = (jax.nn.silu(both[:, :512]) * both[:, 512:]).astype(jnp.bfloat16)
    hidden_ref[...] = hidden
    for i in range(8):
        out_ref[i] = jnp.dot(
            hidden, columns_of(w_ref, i, 1 - where_ref[0]), preferred_element_type=jnp.float32
        ).astype(jnp.bfloat16)
    side = where_ref[1]
    packed = far_ref[144:]
    back = jnp.concatenate([packed[:, 128 * i : 128 * i + 128] for i in range(8)], axis=0)
    kept = own_ref[where_ref[2], pl.ds(pl.multiple_of(side * 128, 128), 128)]
    stream_ref[:, :128] = jnp.where(side == 0, kept, back)
    stream_ref[:, 128:] = jnp.where(side == 0, back, kept)


def down_near_kernel(where_ref, hidden_ref, w_ref, out_ref):
    for i in range(8):
        out_ref[i] = jnp.dot(
            hidden_ref[...], columns_of(w_ref, i, where_ref[0]), preferred_element_type=jnp.float32
        )


def local_call(kernel, where, operands, outs, flops, scratch=()):
    outs = [jax.ShapeDtypeStruct(shape, dtype) for shape, dtype in outs]
    return pl.pallas_call(
        kernel,
        in_specs=[pl.BlockSpec(memory_space=pltpu.SMEM)]
        + [pl.BlockSpec(memory_space=pltpu.VMEM)] * len(operands),
        out_specs=[pl.BlockSpec(memory_space=pltpu.VMEM)] * len(outs),
        out_shape=outs,
        scratch_shapes=scratch,
        compiler_params=pltpu.CompilerParams(vmem_limit_bytes=16 * 1024 * 1024),
        cost_estimate=pl.CostEstimate(flops=flops, bytes_accessed=2**21, transcendentals=0),
    )(where, *operands)


def on_device(
    q_stream,
    k_stream,
    v_stream,
    long_filter,
    skip_gain,
    residual,
    norm_gain,
    w_out,
    w_gate,
    w_up,
    w_down,
):
    side = lax.axis_index("xl")
    core = lax.axis_index("core")
    column = lax.axis_index(("y", "xh"))
    where = jnp.stack([core, side, column]).astype(jnp.int32)
    weights = lax.all_gather(
        jnp.concatenate([w_gate, w_up, w_out], axis=1), "z", axis=0, tiled=True
    ).reshape(8, 2, 128, 1280)

    product = (k_stream.astype(jnp.float32) * v_stream.astype(jnp.float32)).astype(jnp.bfloat16)
    signal = lax.all_to_all(product, ROW, split_axis=0, concat_axis=1, tiled=True)
    length = signal.shape[1]
    tables = dft_tables(length)
    taps = jnp.concatenate([long_filter[:, :1] + skip_gain[:, None], long_filter[:, 1:]], axis=1)
    filter_re, filter_im = forward_dft(taps, tables)
    signal_re, signal_im = forward_dft(signal.astype(jnp.float32), tables)
    joint_re = signal_re * filter_re - signal_im * filter_im
    joint_im = signal_re * filter_im + signal_im * filter_re
    convolved = inverse_dft(joint_re, joint_im, tables, length).astype(jnp.bfloat16)
    convolved = lax.all_to_all(convolved, ROW, split_axis=1, concat_axis=0, tiled=True)
    gated = (q_stream.astype(jnp.float32) * convolved.astype(jnp.float32)).astype(jnp.bfloat16)
    gains = lax.dynamic_index_in_dim(norm_gain.reshape(8, 2, 2, 128), side, 2, keepdims=False)
    gain_own = lax.dynamic_index_in_dim(gains, core, 1, keepdims=False).reshape(1, 1024)
    gain_other = lax.dynamic_index_in_dim(gains, 1 - core, 1, keepdims=False).reshape(1, 1024)
    gated, gain_own, gain_other = lax.optimization_barrier((gated, gain_own, gain_other))
    halves = gated.T.reshape(128, 2, 128).transpose(1, 0, 2)[:, None]
    own = gather_plane(jnp.broadcast_to(halves, (2, 8, 128, 128)).reshape(16, 128, 128))
    other = swap(own, "core")
    mixed = local_call(
        mix_kernel,
        where,
        (
            own,
            other,
            residual.T,
            weights[:, :, :, 1024:],
        ),
        [((2, 256, 128), jnp.bfloat16)],
        2 * 256 * 256 * 2048,
        [pltpu.VMEM((256, 256), jnp.float32)],
    )[0]
    spread = jnp.broadcast_to(mixed[None, :, None], (4, 2, 2, 256, 128)).reshape(16, 256, 128)
    pairs = lax.all_to_all(spread, ("y", "xl", "xh"), split_axis=0, concat_axis=0, tiled=True)
    weights = after(weights, pairs)
    pairs = pairs.reshape(4, 2, 2, 256, 128)
    own = (pairs[:, 0].astype(jnp.float32) + pairs[:, 1].astype(jnp.float32)).astype(jnp.bfloat16)
    own = own.reshape(8, 256, 128)
    other = swap(own, "core")
    begun, power = local_call(
        first_kernel,
        where,
        (own, gain_own, weights),
        [((256, 1024), jnp.float32), ((256, 128), jnp.float32)],
        2 * 256 * 1024 * 1024,
    )
    other = after(other, begun)
    far = local_call(
        far_kernel,
        where,
        (other, gain_other, begun, power, own, weights),
        [((160, 1024), jnp.bfloat16)],
        2 * 128 * 1024 * 1024,
    )[0]
    near, power = local_call(
        near_kernel,
        where,
        (other, gain_other, begun, power, weights),
        [((128, 1024), jnp.float32), ((128, 128), jnp.float32)],
        2 * 128 * 1024 * 1024,
    )
    far = swap(far, "xl")
    far = after(far, near)
    far, hidden, stream = local_call(
        down_far_kernel,
        where,
        (near, far, power, own, w_down),
        [((8, 128, 256), jnp.bfloat16), ((128, 512), jnp.bfloat16), ((128, 256), jnp.bfloat16)],
        2 * 128 * 512 * 2048,
    )
    far = swap(far, "core")
    (near,) = local_call(
        down_near_kernel,
        where,
        (hidden, w_down),
        [((8, 128, 256), jnp.float32)],
        2 * 128 * 512 * 2048,
    )
    far = after(far, near)
    down = (near + far.astype(jnp.float32)).astype(jnp.bfloat16)
    parts = lax.all_to_all(
        down,
        ("xh", "y"),
        split_axis=0,
        concat_axis=0,
        tiled=True,
    )
    down_out = jnp.sum(parts.astype(jnp.float32), axis=0)
    return (stream.astype(jnp.float32) + down_out).astype(jnp.bfloat16).T


def solution(mesh):
    fine = Mesh(mesh.devices.reshape(16, 2, 4, 2, 2), ("z", "xl", "y", "xh", "core"))
    placed = (
        P(COL, ROW),
        P(COL, ROW),
        P(COL, ROW),
        P(COL + ROW, None),
        P(COL + ROW),
        P(COL, ROW),
        P(),
        P(ROW, COL),
        P(ROW, COL),
        P(ROW, COL),
        P(COL, None),
    )
    return jax.shard_map(
        on_device, mesh=fine, in_specs=placed, out_specs=P(COL, ROW), check_vma=False
    )
```
